32 devices in a mesh: groups: 1, expert: 8 (over z, y), dp: 4 (over x, core).
Axes of the slice: x: 2, y: 2, z: 4, core: 2. Of those that a mesh axis runs over, the one named last changes fastest.
Arguments:
- queries: bfloat16 [2048, 4096], P(('groups', 'dp'), 'expert'), may hold values from -6 to 6
- keys_in: bfloat16 [2048, 4096], P(('groups', 'dp'), 'expert'), may hold values from -6 to 6
- values_in: bfloat16 [2048, 4096], P(('groups', 'dp'), 'expert'), may hold values from -6 to 6
- gate_in: bfloat16 [2048, 4096], P(('groups', 'dp'), 'expert'), may hold values from -6 to 6
- beta: float32 [2048, 32], P(('groups', 'dp'), 'expert'), may hold values from 0.1 to 1
- decay: float32 [2048, 32], P(('groups', 'dp'), 'expert'), may hold values from -1 to 0
- lengths: int32 [4, 4], P(('groups', 'dp')), may hold values from 1 to 256, 512 in all within a row
- cache: float32 [16, 32, 128, 128], P(('groups', 'dp'), 'expert'), may hold values from -6 to 6
- norm_gain: float32 [128], replicated, may hold values from 0.1 to 1.9
- out_proj: bfloat16 [4096, 2048], P('expert'), may hold values from -0.09375 to 0.09375
- residual: bfloat16 [2048, 2048], P(('groups', 'dp', 'expert')), may hold values from -6 to 6
- post_gain: float32 [2048], replicated, may hold values from 0.1 to 1.9
- expert_ids: int32 [2048, 10], P(('groups', 'dp', 'expert')), may hold values from 0 to 31, all different within a row; in each aligned block of 64 rows (0 to 63, 64 to 127, ...) at most 25 rows name the same one
- route_weights: float32 [2048, 10], P(('groups', 'dp', 'expert')), may hold values from 0.05 to 1
- gate_up: bfloat16 [32, 2048, 512], P(('expert', 'dp')), may hold values from -0.125 to 0.125
- down_proj: bfloat16 [32, 256, 2048], P(('expert', 'dp')), may hold values from -0.375 to 0.375
Outputs:
- moe_out: bfloat16 [2048, 2048], P(('groups', 'dp', 'expert'))
- attn_out: bfloat16 [2048, 2048], P(('groups', 'dp', 'expert'))
- new_states: float32 [16, 32, 128, 128], P(('groups', 'dp'), 'expert')
The draws below stay inside these ranges and needn't reach their ends.
Inputs may be any that keep to these rules, and one draw needn't show every extreme that they name: Each row of lengths fills its shard's 512 rows; the longest span of each row is exactly 256. `expert_ids`: each row names 10 different experts. Within the 64 rows of one device no expert is named more than 25 times, a bound that some block reaches; every expert is named somewhere.
All inputs are finite; a program needn't handle non-finite values.
Results may differ from the reference program's by a relative error of at most 0.025.
Values may be sent and summed in bfloat16 or wider, within the bound.
A program may use at most 64 MiB of HBM per device.

```python
import math
import jax
import jax.numpy as jnp
import numpy as np
from jax import lax

D = 2048
HEAD = 128
VALUE_HEADS = 32
TOP = 10
FF = 256
SPAN_MAX = 256
TOK_DP = 512
REQ_DP = 4
TOK_DEV = 64
TOKEN_ROWS_ALL = 2048
REQS = 16
SHARDS = 4
EXPERTS = 32
CAP = 25
N_EXPERT = 8
N_DP = 4


def draw_decay(key, part):
    base = jax.random.fold_in(key, 11)
    request_flows = jax.random.split(base, 6)
    share = 0.4
    fast = jax.random.uniform(request_flows[0], (VALUE_HEADS,)) < share
    fast_rate = jnp.exp(jax.random.uniform(request_flows[1], (VALUE_HEADS,), minval=math.log(1.0 / 50.0), maxval=math.log(1.0 / 30.0)))
    slow_rate = jnp.exp(jax.random.uniform(request_flows[2], (VALUE_HEADS,), minval=math.log(0.001), maxval=math.log(0.004)))
    arrival_rates = jnp.where(fast, fast_rate, slow_rate)
    random_wobble = jnp.exp(jax.random.uniform(request_flows[3], (TOKEN_ROWS_ALL, VALUE_HEADS), minval=math.log(0.5), maxval=math.log(2.0)))
    surge_token_rows = jax.random.uniform(request_flows[4], (TOKEN_ROWS_ALL, 1)) < 1.0 / 64.0
    surge_length = jax.random.uniform(request_flows[5], (TOKEN_ROWS_ALL, VALUE_HEADS), minval=0.22, maxval=0.7)
    grand_count = arrival_rates[None, :] * random_wobble + jnp.where(surge_token_rows, surge_length, 0.0)
    return (-grand_count).astype(jnp.float32)


def level_of(key, dims, cuts, smallest, high):
    def one(position, blocks):
        steps = jax.random.uniform(jax.random.fold_in(jax.random.fold_in(key, 6), position), (blocks,), jnp.float32, smallest / len(cuts), high / len(cuts))
        return jnp.repeat(jnp.exp(steps), dims[position] // blocks).reshape((-1,) + (1,) * (len(dims) - position - 1))

    level = one(*cuts[0])
    for cut in cuts[1:]:
        level = level * one(*cut)
    return level


def length_profile(count, total, most, lean):
    portions = [(1 << 20) // math.isqrt(grade ** lean) + 1 for grade in range(2, count + 1)]
    surplus, given = total - most - (count - 1), [1] * (count - 1)
    while surplus > 0:
        movable = [i for i in range(count - 1) if given[i] < most]
        mass, left = sum([portions[i] for i in movable]), surplus
        for i in movable:
            more = min(most - given[i], max(1, left * portions[i] // mass), surplus)
            given[i] = given[i] + more
            surplus = surplus - more
    return np.array([most] + given)


def ragged(key, count, total, reach, slope):
    if count == 2:
        one = jax.random.randint(key, (), max(1, total - reach), min(reach, total - 1) + 1)
        return jnp.stack([one, total - one])
    sizes = jnp.asarray(length_profile(count, total, reach, slope), jnp.int32)
    twos = (count - 1) // 2
    giver, receiver = sizes[1:1 + 2 * twos:2], sizes[2:2 + 2 * twos:2]
    room = jnp.minimum(giver - 1, reach - receiver)
    shifted = jax.random.randint(jax.random.fold_in(key, 1), (twos,), 0, 1 << 20) % (room + 1)
    sizes = sizes.at[1:1 + 2 * twos:2].set(giver - shifted).at[2:2 + 2 * twos:2].set(receiver + shifted)
    return sizes[jax.random.permutation(jax.random.fold_in(key, 2), count)]


def shared_out(stream_key, own, number, rows, count, top, bound, lean):
    order = jax.random.permutation(stream_key, count)
    heavy_load, ordinary = shares(count, rows * top, bound, lean, True), shares(count, rows * top, bound, lean, False)
    places = jnp.arange(count)

    def named(sizes, offset_by):
        used = int((sizes > 0).sum())
        fixed = max(1, used // 4)
        passed = fixed + (places - fixed + offset_by * (used - fixed)) % max(1, count - fixed)
        return jnp.zeros((count,), jnp.int32).at[order[jnp.where(places < fixed, places, passed)]].set(jnp.asarray(sizes, jnp.int32))

    sizes = jnp.where(number % 4 == 0, named(heavy_load, number // 4), named(ordinary, number - number // 4 - 1))
    mixed = jax.random.permutation(jax.random.fold_in(own, 3), count)
    giver, taker = mixed[0:count // 2 * 2:2], mixed[1:count // 2 * 2:2]
    slack = jnp.minimum(sizes[giver] - 1, bound - sizes[taker]) // 2
    slack = jnp.where((giver == order[0]) | (taker == order[0]) | (sizes[taker] == 0), 0, jnp.maximum(slack, 0))
    passed = jax.random.randint(jax.random.fold_in(own, 4), (count // 2,), 0, 1 << 20) % (slack + 1)
    sizes = sizes.at[giver].add(-passed).at[taker].add(passed)
    labels = jnp.searchsorted(jnp.cumsum(sizes), jnp.arange(rows * top), side="right").astype(jnp.int32)
    listing = labels.reshape(top, rows).T
    listing = listing[jax.random.permutation(jax.random.fold_in(own, 1), rows)]
    offset_by = jax.random.randint(jax.random.fold_in(own, 2), (rows, 1), 0, top)
    return jnp.take_along_axis(listing, (jnp.arange(top)[None, :] + offset_by) % top, axis=1)


def shares(number_of, total, bound, slope, full):
    weights = [(1 << 20) // math.isqrt(standing ** slope) + 1 for standing in range(1, number_of + 1)]
    largest = bound if full else min(bound, max(-(-total // number_of), total * weights[0] // sum(weights)))
    least = 1 if total - largest >= number_of - 1 else 0
    holding, spare = [largest] + [least] * (number_of - 1), total - largest - least * (number_of - 1)
    while spare > 0:
        candidates = [i for i in range(1, number_of) if holding[i] < largest] or [i for i in range(1, number_of) if holding[i] < bound]
        whole, left = sum([weights[i] for i in candidates]), spare
        for i in candidates:
            extra = min(bound - holding[i], max(1, left * weights[i] // whole), spare)
            holding[i] = holding[i] + extra
            spare = spare - extra
    return np.array(holding)


def normal_values(own_key, extent, spread, most, cuts=(), held_as=jnp.bfloat16):
    entries = jax.random.normal(own_key, extent, jnp.float32) * spread
    if len(cuts) > 0:
        entries = level_of(own_key, extent, cuts, -0.22, 0.18) * entries
    return jnp.clip(entries, min=-most, max=most).astype(held_as)


def setup_inputs(seed: int = 0, part: int = 0) -> dict:
    streams_of = jax.random.split(jax.random.key(seed), 17)
    part_splits = jax.random.split(jax.random.fold_in(streams_of[16], part), 17)
    queries = normal_values(part_splits[0], (TOKEN_ROWS_ALL, VALUE_HEADS * HEAD), 1.0, 6.0, ((0, 4), (1, 8)))
    keys_in = normal_values(part_splits[1], (TOKEN_ROWS_ALL, VALUE_HEADS * HEAD), 1.0, 6.0, ((0, 4), (1, 8)))
    values_in = normal_values(part_splits[2], (TOKEN_ROWS_ALL, VALUE_HEADS * HEAD), 1.0, 6.0, ((0, 4), (1, 8)))
    gate_in = normal_values(part_splits[3], (TOKEN_ROWS_ALL, VALUE_HEADS * HEAD), 1.0, 6.0, ((0, 4), (1, 8)))
    beta = jnp.clip(0.1 + 0.9 * jax.random.uniform(part_splits[4], (TOKEN_ROWS_ALL, VALUE_HEADS), jnp.float32) ** level_of(part_splits[4], (TOKEN_ROWS_ALL, VALUE_HEADS), ((0, 4), (1, 8)), -0.2, 0.2), 0.1, 1.0)
    decay = draw_decay(jax.random.fold_in(jax.random.fold_in(streams_of[16], part), 71), part)
    lengths = jax.vmap(lambda own: ragged(own, REQ_DP, TOK_DP, SPAN_MAX, 2))(jax.random.split(part_splits[6], SHARDS)).reshape((SHARDS, REQ_DP)).astype(jnp.int32)
    cache = normal_values(part_splits[7], (REQS, VALUE_HEADS, HEAD, HEAD), 1.0, 6.0, ((0, 4), (1, 8)), jnp.float32)
    norm_gain = jnp.clip(1.0 + 0.18 * jax.random.normal(streams_of[8], (HEAD,), jnp.float32), 0.1, 1.9)
    out_proj = normal_values(streams_of[9], (VALUE_HEADS * HEAD, D), (VALUE_HEADS * HEAD) ** -0.5, 0.09375, ((0, 8),))
    residual = normal_values(part_splits[10], (TOKEN_ROWS_ALL, D), 1.0, 6.0, ((0, 32),))
    post_gain = jnp.clip(1.0 + 0.18 * jax.random.normal(streams_of[11], (D,), jnp.float32), 0.1, 1.9)
    expert_ids_keys = jax.random.split(jax.random.fold_in(part_splits[12], 1), TOKEN_ROWS_ALL // TOK_DEV)
    expert_ids_turns = jax.random.permutation(jax.random.fold_in(part_splits[12], 3), TOKEN_ROWS_ALL // TOK_DEV)
    expert_ids = jax.vmap(lambda own, number: shared_out(jax.random.fold_in(part_splits[12], 2), own, number, TOK_DEV, EXPERTS, TOP, CAP, 2))(expert_ids_keys, expert_ids_turns).reshape((TOKEN_ROWS_ALL, TOP))
    route_weights = jnp.clip(jnp.exp(math.log(1.0) - 2.9957323 * jax.random.uniform(part_splits[13], (TOKEN_ROWS_ALL, TOP), jnp.float32) ** level_of(part_splits[13], (TOKEN_ROWS_ALL, TOP), ((0, 32),), -0.2, 0.2)), 0.05, 1.0)
    gate_up = normal_values(streams_of[14], (EXPERTS, D, 2 * FF), D ** -0.5, 0.125, ((0, 32),))
    down_proj = normal_values(streams_of[15], (EXPERTS, FF, D), FF ** -0.5, 0.375, ((0, 32),))
    return dict(queries=queries, keys_in=keys_in, values_in=values_in, gate_in=gate_in, beta=beta, decay=decay, lengths=lengths, cache=cache, norm_gain=norm_gain, out_proj=out_proj, residual=residual, post_gain=post_gain, expert_ids=expert_ids, route_weights=route_weights, gate_up=gate_up, down_proj=down_proj)


HIGH = lax.Precision.HIGHEST
epsilon = 1e-06

def unit_rows(values):
    return values * lax.rsqrt(lax.optimization_barrier(jnp.sum(values * values, axis=-1, keepdims=True)) + epsilon)

def reference(queries, keys_in, values_in, gate_in, beta, decay, lengths, cache, norm_gain, out_proj, residual, post_gain, expert_ids, route_weights, gate_up, down_proj):
    shards = lengths.shape[0]
    layout = (shards, TOK_DP, VALUE_HEADS, HEAD)
    query_n = unit_rows(queries.astype(jnp.float32).reshape(layout)) * HEAD ** (-0.5)
    key_n = unit_rows(keys_in.astype(jnp.float32).reshape(layout))
    value_f = values_in.astype(jnp.float32).reshape(layout)
    beta_s = beta.reshape(shards, TOK_DP, VALUE_HEADS)
    decay_s = decay.reshape(shards, TOK_DP, VALUE_HEADS)
    ends = jnp.cumsum(lengths, axis=1).astype(jnp.int32)
    starts = (ends - lengths).astype(jnp.int32)
    places = jnp.arange(TOK_DP, dtype=jnp.int32)
    request = lax.optimization_barrier(jnp.sum((places[None, :, None] >= ends[:, None, :]).astype(jnp.int32), axis=2)).astype(jnp.int32)
    first_row = jnp.any(places[None, :, None] == starts[:, None, :], axis=2)
    last_row = jnp.any(places[None, :, None] == ends[:, None, :] - 1, axis=2)
    initial = cache.reshape(shards, REQ_DP, VALUE_HEADS, HEAD, HEAD)
    shard_rows = jnp.arange(shards, dtype=jnp.int32)

    def token_step(carry, item):
        memory, finals = carry
        query_t, key_t, value_t, beta_t, decay_t, request_t, first_t, last_t = item
        memory = jnp.where(first_t[:, None, None, None], initial[shard_rows, request_t], memory)
        recalled = jnp.einsum('dhk,dhkv->dhv', key_t, memory, precision=HIGH)
        keep = jnp.exp(decay_t)[:, :, None, None]
        write = beta_t[:, :, None, None]
        memory = keep * (memory - write * key_t[..., None] * recalled[:, :, None, :]) + write * key_t[..., None] * value_t[:, :, None, :]
        mixed = jnp.einsum('dhk,dhkv->dhv', query_t, memory, precision=HIGH)
        previous = finals[shard_rows, request_t]
        finals = finals.at[shard_rows, request_t].set(jnp.where(last_t[:, None, None, None], memory, previous))
        return ((memory, finals), mixed)

    def rows_first(array):
        return jnp.swapaxes(array, 0, 1)
    start_memory = jnp.zeros((shards, VALUE_HEADS, HEAD, HEAD), jnp.float32)
    inputs = (rows_first(query_n), rows_first(key_n), rows_first(value_f), rows_first(beta_s), rows_first(decay_s), rows_first(request), rows_first(first_row), rows_first(last_row))
    (unused, finals), mixed = lax.scan(token_step, (start_memory, initial), inputs)
    mixed = rows_first(mixed).reshape(TOKEN_ROWS_ALL, VALUE_HEADS, HEAD)
    new_states = finals.reshape(REQS, VALUE_HEADS, HEAD, HEAD)
    gate_f = gate_in.astype(jnp.float32).reshape(TOKEN_ROWS_ALL, VALUE_HEADS, HEAD)
    scale = lax.rsqrt(lax.optimization_barrier(jnp.mean(mixed * mixed, axis=-1, keepdims=True)) + epsilon)
    normed = (mixed * scale * norm_gain * jax.nn.silu(gate_f)).astype(jnp.bfloat16).reshape(TOKEN_ROWS_ALL, VALUE_HEADS * HEAD)
    attn = jnp.dot(normed, out_proj, preferred_element_type=jnp.float32)
    attn_out = (residual.astype(jnp.float32) + attn).astype(jnp.bfloat16)
    stream = attn_out.astype(jnp.float32)
    routed = (stream * lax.rsqrt(lax.optimization_barrier(jnp.mean(stream * stream, axis=-1, keepdims=True)) + epsilon) * post_gain).astype(jnp.bfloat16)
    flat_ids = expert_ids.reshape(-1).astype(jnp.int32)
    flat_weights = route_weights.reshape(-1)
    order = jnp.argsort(flat_ids, stable=True).astype(jnp.int32)
    counts = lax.optimization_barrier(jnp.sum((flat_ids[:, None] == jnp.arange(EXPERTS, dtype=jnp.int32)[None, :]).astype(jnp.int32), axis=0)).astype(jnp.int32)
    offsets = (jnp.cumsum(counts) - counts).astype(jnp.int32)
    limit = N_EXPERT * N_DP * CAP
    padded = jnp.concatenate([order, jnp.zeros((limit,), jnp.int32)])

    def expert_step(grand_count, item):
        number, weights_gu, weights_down = item
        picked = lax.dynamic_slice_in_dim(padded, offsets[number].astype(jnp.int32), limit).astype(jnp.int32)
        valid = jnp.arange(limit, dtype=jnp.int32) < counts[number]
        token_of = (picked // TOP).astype(jnp.int32)
        inputs_e = routed[token_of]
        both = jnp.dot(inputs_e, weights_gu, preferred_element_type=jnp.float32)
        hidden = (jax.nn.silu(both[:, :FF]) * both[:, FF:]).astype(jnp.bfloat16)
        result = jnp.dot(hidden, weights_down, preferred_element_type=jnp.float32).astype(jnp.bfloat16)
        weighted = jnp.where(valid[:, None], result.astype(jnp.float32) * flat_weights[picked][:, None], 0.0)
        return (grand_count.at[token_of].add(weighted), None)
    numbers = jnp.arange(EXPERTS, dtype=jnp.int32)
    grand_count, unused2 = lax.scan(expert_step, jnp.zeros((TOKEN_ROWS_ALL, D), jnp.float32), (numbers, gate_up, down_proj))
    moe_out = grand_count.astype(jnp.bfloat16)
    return (moe_out, attn_out, new_states)
```

```python
import jax
import jax.numpy as jnp
from jax import lax
from jax.sharding import PartitionSpec as P

HIGH = lax.Precision.HIGHEST
epsilon = 1e-06
block_rows = 64


def unit_rows(values):
    return values * lax.rsqrt(jnp.sum(values * values, axis=-1, keepdims=True) + epsilon)


def block_step(states, item):
    query_b, key_b, value_b, beta_b, decay_b, member_b = item
    size = query_b.shape[0]
    places = jnp.arange(size)
    shared = jnp.dot(member_b, member_b.T, precision=HIGH) > 0.5
    inside = shared & (places[:, None] >= places[None, :])
    strict_part = inside & (places[:, None] > places[None, :])
    running = jnp.dot(inside.astype(jnp.float32), decay_b, precision=HIGH).T
    log_gaps = running[:, :, None] - running[:, None, :]
    decays = jnp.where(inside[None], jnp.exp(jnp.minimum(log_gaps, 0.0)), 0.0)
    key_h = jnp.swapaxes(key_b, 0, 1)
    query_h = jnp.swapaxes(query_b, 0, 1)
    value_h = jnp.swapaxes(value_b, 0, 1)
    beta_h = beta_b.T
    key_dots = jnp.einsum("hik,hjk->hij", key_h, key_h, precision=HIGH)
    strict_terms = jnp.where(strict_part[None], decays * key_dots * beta_h[:, :, None], 0.0)
    identity = jnp.eye(size, dtype=jnp.float32)[None]
    inverse = identity - strict_terms
    powered = strict_terms
    covered = 2
    while covered < size:
        powered = jnp.einsum("hij,hjk->hik", powered, powered, precision=HIGH)
        inverse = jnp.einsum("hij,hjk->hik", inverse, identity + powered, precision=HIGH)
        covered = covered * 2
    growth = jnp.exp(running)
    targets = jnp.concatenate(
        [key_h * (beta_h * growth)[:, :, None], value_h * beta_h[:, :, None]], axis=2
    )
    solved = jnp.einsum("hij,hjc->hic", inverse, targets, precision=HIGH)
    width = key_h.shape[2]
    key_mix = solved[:, :, :width]
    value_mix = solved[:, :, width:]
    recalled = jnp.einsum("hck,hrkv->hrcv", key_mix, states, precision=HIGH)
    recalled = jnp.einsum("cr,hrcv->hcv", member_b, recalled, precision=HIGH)
    updates = value_mix - recalled
    from_state = jnp.einsum("hck,hrkv->hrcv", query_h, states, precision=HIGH)
    from_state = jnp.einsum("cr,hrcv->hcv", member_b, from_state, precision=HIGH)
    query_dots = jnp.einsum("hik,hjk->hij", query_h, key_h, precision=HIGH)
    mixed = growth[:, :, None] * from_state + jnp.einsum(
        "hij,hjv->hiv", query_dots * decays, updates, precision=HIGH
    )
    span_total = jnp.einsum("cr,ch->hr", member_b, decay_b, precision=HIGH)
    end_gaps = span_total[:, :, None] - running[:, None, :]
    carried = jnp.where(member_b.T[None] > 0.5, jnp.exp(jnp.minimum(end_gaps, 0.0)), 0.0)
    fresh = jnp.einsum("hrc,hck,hcv->hrkv", carried, key_h, updates, precision=HIGH)
    states = jnp.exp(span_total)[:, :, None, None] * states + fresh
    return (states, jnp.swapaxes(mixed, 0, 1))


def on_device(
    queries,
    keys_in,
    values_in,
    gate_in,
    beta,
    decay,
    lengths,
    cache,
    norm_gain,
    out_proj,
    residual,
    post_gain,
    expert_ids,
    route_weights,
    gate_up,
    down_proj,
):
    tok_count = queries.shape[0]
    experts_all = lax.axis_size("expert") * lax.axis_size("dp")
    own_expert = lax.axis_index("expert") * lax.axis_size("dp") + lax.axis_index("dp")
    named = expert_ids[:, :, None] == jnp.arange(experts_all, dtype=jnp.int32)[None, None, :]
    spread = jnp.sum(jnp.where(named, route_weights[:, :, None], 0.0), axis=1)
    spread = lax.all_gather(spread, ("dp", "expert"), axis=0, tiled=True)
    own_weight = lax.dynamic_slice_in_dim(spread, own_expert, 1, axis=1)
    heads = beta.shape[1]
    head_dim = norm_gain.shape[0]
    requests = lengths.shape[1]
    block = min(block_rows, tok_count)
    blocks = tok_count // block
    layout = (blocks, block, heads, head_dim)
    query_n = unit_rows(queries.astype(jnp.float32).reshape(layout)) * head_dim ** (-0.5)
    key_n = unit_rows(keys_in.astype(jnp.float32).reshape(layout))
    value_f = values_in.astype(jnp.float32).reshape(layout)
    upto = jnp.arange(requests)[:, None] >= jnp.arange(requests)[None, :]
    ends = jnp.sum(jnp.where(upto, lengths[0][None, :], 0), axis=1)
    places = jnp.arange(tok_count, dtype=jnp.int32)
    request = jnp.sum((places[:, None] >= ends[None, :]).astype(jnp.int32), axis=1)
    member = (request[:, None] == jnp.arange(requests, dtype=jnp.int32)[None, :]).astype(
        jnp.float32
    )
    inputs = (
        query_n,
        key_n,
        value_f,
        beta.reshape(blocks, block, heads),
        decay.reshape(blocks, block, heads),
        member.reshape(blocks, block, requests),
    )
    states, mixed = lax.scan(block_step, jnp.swapaxes(cache, 0, 1), inputs)
    new_states = jnp.swapaxes(states, 0, 1)
    mixed = mixed.reshape(tok_count, heads, head_dim)
    gate_f = gate_in.astype(jnp.float32).reshape(tok_count, heads, head_dim)
    scale = lax.rsqrt(jnp.mean(mixed * mixed, axis=-1, keepdims=True) + epsilon)
    normed = (
        (mixed * scale * norm_gain * jax.nn.silu(gate_f))
        .astype(jnp.bfloat16)
        .reshape(tok_count, heads * head_dim)
    )
    tok_local = residual.shape[0]
    attn = lax.psum_scatter(
        jnp.dot(normed, out_proj, preferred_element_type=jnp.float32).astype(jnp.bfloat16),
        "expert",
        scatter_dimension=0,
        tiled=True,
    ).astype(jnp.float32)
    attn_out = (residual.astype(jnp.float32) + attn).astype(jnp.bfloat16)
    stream = attn_out.astype(jnp.float32)
    routed = (
        stream * lax.rsqrt(jnp.mean(stream * stream, axis=-1, keepdims=True) + epsilon) * post_gain
    ).astype(jnp.bfloat16)
    rows = lax.all_gather(routed, ("dp", "expert"), axis=0, tiled=True)
    both = jnp.dot(rows, gate_up[0], preferred_element_type=jnp.float32)
    hidden_width = down_proj.shape[1]
    hidden = (jax.nn.silu(both[:, :hidden_width]) * both[:, hidden_width:]).astype(jnp.bfloat16)
    result = jnp.dot(hidden, down_proj[0], preferred_element_type=jnp.float32)
    share = (result * own_weight).astype(jnp.bfloat16)
    moe_out = lax.psum_scatter(share, ("dp", "expert"), scatter_dimension=0, tiled=True)
    return (moe_out, attn_out, new_states)


def solution(mesh):
    return jax.shard_map(
        on_device,
        mesh=mesh,
        in_specs=(
            P(("groups", "dp"), "expert"),
            P(("groups", "dp"), "expert"),
            P(("groups", "dp"), "expert"),
            P(("groups", "dp"), "expert"),
            P(("groups", "dp"), "expert"),
            P(("groups", "dp"), "expert"),
            P(("groups", "dp"), None),
            P(("groups", "dp"), "expert", None, None),
            P(),
            P("expert", None),
            P(("groups", "dp", "expert"), None),
            P(),
            P(("groups", "dp", "expert"), None),
            P(("groups", "dp", "expert"), None),
            P(("expert", "dp"), None, None),
            P(("expert", "dp"), None, None),
        ),
        out_specs=(
            P(("groups", "dp", "expert"), None),
            P(("groups", "dp", "expert"), None),
            P(("groups", "dp"), "expert", None, None),
        ),
        check_vma=False,
    )
```

```python
import jax
import jax.numpy as jnp
from jax import lax
from jax.experimental import pallas as pl
from jax.experimental.pallas import tpu as pltpu
from jax.sharding import PartitionSpec as P

HIGH = lax.Precision.HIGHEST
epsilon = 1e-06
block_rows = 64


def dot(a, b, dims=((1,), (0,))):
    return lax.dot_general(a, b, (dims, ((), ())), preferred_element_type=jnp.float32)


def halves(a):
    high = a.astype(jnp.bfloat16)
    return high, (a - high.astype(jnp.float32)).astype(jnp.bfloat16)


def fine_dot(a, b):
    a_high, a_low = halves(a)
    b_high, b_low = halves(b)
    return dot(a_high, b_high) + (dot(a_high, b_low) + dot(a_low, b_high))


def unit_inverse(lower, row, column):
    size = lower.shape[0]

    def same(width):
        shift = width.bit_length() - 1
        return (row >> shift) == (column >> shift)

    width = min(8, size)
    identity = jnp.where(row == column, 1.0, 0.0)
    first = jnp.where(same(width), lower, 0.0)
    second = fine_dot(first, first)
    fourth = fine_dot(second, second)
    inverse = identity - first
    inverse = inverse + fine_dot(inverse, second)
    inverse = inverse + fine_dot(inverse, fourth)
    while width < size:
        between = jnp.where(same(2 * width) & jnp.logical_not(same(width)), lower, 0.0)
        inverse = inverse - fine_dot(inverse, fine_dot(between, inverse))
        width = 2 * width
    return inverse


def mix_kernel(
    queries, keys, values, gates, beta, decay, decay_t, request, request_t, cache, gain,
    normed, new_states, states,
):
    requests, heads, head_dim, _ = cache.shape
    blocks, _, size = request_t.shape
    for h in range(heads):
        for r in range(requests):
            states[h, :, r * head_dim : (r + 1) * head_dim] = cache[r, h]
    row = lax.broadcasted_iota(jnp.int32, (size, size), 0)
    column = lax.broadcasted_iota(jnp.int32, (size, size), 1)

    def step(block, carry):
        rows = pl.ds(pl.multiple_of(block * size, size), size)
        owner = request[rows, :]
        shared = owner == request_t[block]
        inside = shared & (row >= column)
        strict = shared & (row > column)
        inside_f = inside.astype(jnp.float32)
        decay_b = decay[rows, :]
        running = jnp.dot(inside_f, decay_b, precision=HIGH, preferred_element_type=jnp.float32)
        running_t = lax.dot_general(
            decay_t[block], inside_f, (((1,), (1,)), ((), ())),
            precision=HIGH, preferred_element_type=jnp.float32,
        )
        total = jnp.dot(
            shared.astype(jnp.float32), decay_b,
            precision=HIGH, preferred_element_type=jnp.float32,
        )
        growth_all = jnp.exp(running)
        carried_all = jnp.exp(jnp.minimum(total - running, 0.0))
        beta_b = beta[rows, :]
        for h in range(heads):
            lanes = slice(h * head_dim, (h + 1) * head_dim)
            query, key = queries[rows, lanes], keys[rows, lanes]
            query_f, key_f = query.astype(jnp.float32), key.astype(jnp.float32)
            query_s = lax.rsqrt(jnp.sum(query_f * query_f, axis=1, keepdims=True) + epsilon)
            query_s = query_s * head_dim ** (-0.5)
            key_s = lax.rsqrt(jnp.sum(key_f * key_f, axis=1, keepdims=True) + epsilon)
            growth = growth_all[:, h : h + 1]
            write = beta_b[:, h : h + 1] * key_s
            gaps = running[:, h : h + 1] - running_t[h : h + 1, :]
            decays = jnp.where(inside, jnp.exp(jnp.minimum(gaps, 0.0)), 0.0)
            both = jnp.concatenate([key, query], axis=0)
            dots = dot(both, key, ((1,), (1,)))
            lower = jnp.where(strict, decays * dots[:size] * (write * key_s), 0.0)
            inverse = unit_inverse(lower, row, column)
            state = states[h]
            high, low = halves(state)
            recalled_all = dot(both, high) + dot(both, low)
            recalled = jnp.zeros((size, head_dim), jnp.float32)
            asked = jnp.zeros((size, head_dim), jnp.float32)
            for r in range(requests):
                part = recalled_all[:, r * head_dim : (r + 1) * head_dim]
                recalled = jnp.where(owner == r, part[:size], recalled)
                asked = jnp.where(owner == r, part[size:], asked)
            value = values[rows, lanes].astype(jnp.float32)
            updates = fine_dot(inverse, write * (value - growth * key_s * recalled))
            mixed = growth * asked + dot(
                (decays * dots[size:]).astype(jnp.bfloat16), updates.astype(jnp.bfloat16)
            )
            mixed = mixed * query_s
            kept = carried_all[:, h : h + 1] * updates
            spread = jnp.concatenate(
                [jnp.where(owner == r, kept, 0.0) for r in range(requests)], axis=1
            )
            high, low = halves(spread)
            fresh = dot(key, high, ((0,), (0,))) + dot(key, low, ((0,), (0,)))
            for r in range(requests):
                part = slice(r * head_dim, (r + 1) * head_dim)
                span = jnp.sum(
                    jnp.where(owner == r, decay_b[:, h : h + 1], 0.0), axis=0, keepdims=True
                )
                states[h, :, part] = jnp.exp(span) * state[:, part] + fresh[:, part]
            gate = gates[rows, lanes].astype(jnp.float32)
            scale = lax.rsqrt(jnp.mean(mixed * mixed, axis=1, keepdims=True) + epsilon)
            normed[rows, lanes] = (mixed * scale * gain[...] * jax.nn.silu(gate)).astype(
                jnp.bfloat16
            )
        return carry

    lax.fori_loop(0, blocks, step, 0)
    for h in range(heads):
        for r in range(requests):
            new_states[r, h] = states[h, :, r * head_dim : (r + 1) * head_dim]


def on_device(
    queries,
    keys_in,
    values_in,
    gate_in,
    beta,
    decay,
    lengths,
    cache,
    norm_gain,
    out_proj,
    residual,
    post_gain,
    expert_ids,
    route_weights,
    gate_up,
    down_proj,
):
    tok_count = queries.shape[0]
    experts_all = lax.axis_size("expert") * lax.axis_size("dp")
    own_expert = lax.axis_index("expert") * lax.axis_size("dp") + lax.axis_index("dp")
    named = expert_ids[:, :, None] == jnp.arange(experts_all, dtype=jnp.int32)[None, None, :]
    spread = jnp.sum(jnp.where(named, route_weights[:, :, None], 0.0), axis=1)
    spread = lax.all_gather(spread, ("dp", "expert"), axis=0, tiled=True)
    own_weight = lax.dynamic_slice_in_dim(spread, own_expert, 1, axis=1)
    heads = beta.shape[1]
    head_dim = norm_gain.shape[0]
    requests = lengths.shape[1]
    block = min(block_rows, tok_count)
    blocks = tok_count // block
    upto = jnp.arange(requests)[:, None] >= jnp.arange(requests)[None, :]
    ends = jnp.sum(jnp.where(upto, lengths[0][None, :], 0), axis=1)
    places = jnp.arange(tok_count, dtype=jnp.int32)
    request = jnp.sum((places[:, None] >= ends[None, :]).astype(jnp.int32), axis=1)
    normed, new_states = pl.pallas_call(
        mix_kernel,
        out_shape=(
            jax.ShapeDtypeStruct(queries.shape, jnp.bfloat16),
            jax.ShapeDtypeStruct(cache.shape, jnp.float32),
        ),
        in_specs=[pl.BlockSpec(memory_space=pltpu.VMEM)] * 11,
        out_specs=[pl.BlockSpec(memory_space=pltpu.VMEM)] * 2,
        scratch_shapes=[pltpu.VMEM((heads, head_dim, requests * head_dim), jnp.float32)],
        compiler_params=pltpu.CompilerParams(vmem_limit_bytes=40 * 1024 * 1024),
    )(
        queries,
        keys_in,
        values_in,
        gate_in,
        beta,
        decay,
        jnp.swapaxes(decay.reshape(blocks, block, heads), 1, 2),
        request[:, None],
        request.reshape(blocks, 1, block),
        cache,
        norm_gain[None, :],
    )
    tok_local = residual.shape[0]
    attn = lax.psum_scatter(
        jnp.dot(normed, out_proj, preferred_element_type=jnp.float32).astype(jnp.bfloat16),
        "expert",
        scatter_dimension=0,
        tiled=True,
    ).astype(jnp.float32)
    attn_out = (residual.astype(jnp.float32) + attn).astype(jnp.bfloat16)
    stream = attn_out.astype(jnp.float32)
    routed = (
        stream * lax.rsqrt(jnp.mean(stream * stream, axis=-1, keepdims=True) + epsilon) * post_gain
    ).astype(jnp.bfloat16)
    rows = lax.all_gather(routed, ("dp", "expert"), axis=0, tiled=True)
    both = jnp.dot(rows, gate_up[0], preferred_element_type=jnp.float32)
    hidden_width = down_proj.shape[1]
    hidden = (jax.nn.silu(both[:, :hidden_width]) * both[:, hidden_width:]).astype(jnp.bfloat16)
    result = jnp.dot(hidden, down_proj[0], preferred_element_type=jnp.float32)
    share = (result * own_weight).astype(jnp.bfloat16)
    share = lax.psum_scatter(share, "dp", scatter_dimension=0, tiled=True)
    moe_out = lax.psum_scatter(share, "expert", scatter_dimension=0, tiled=True)
    return (moe_out, attn_out, new_states)


def solution(mesh):
    return jax.shard_map(
        on_device,
        mesh=mesh,
        in_specs=(
            P(("groups", "dp"), "expert"),
            P(("groups", "dp"), "expert"),
            P(("groups", "dp"), "expert"),
            P(("groups", "dp"), "expert"),
            P(("groups", "dp"), "expert"),
            P(("groups", "dp"), "expert"),
            P(("groups", "dp"), None),
            P(("groups", "dp"), "expert", None, None),
            P(),
            P("expert", None),
            P(("groups", "dp", "expert"), None),
            P(),
            P(("groups", "dp", "expert"), None),
            P(("groups", "dp", "expert"), None),
            P(("expert", "dp"), None, None),
            P(("expert", "dp"), None, None),
        ),
        out_specs=(
            P(("groups", "dp", "expert"), None),
            P(("groups", "dp", "expert"), None),
            P(("groups", "dp"), "expert", None, None),
        ),
        check_vma=False,
    )
```
